512 devices in a mesh: row: 16 (over z_lo, core), col: 32 (over x, z_hi, y).
Axes of the slice: x: 4, y: 4, z: 16 (z_hi: 2, z_lo: 8; z = z_hi * 8 + z_lo), core: 2. Of those that a mesh axis runs over, the one named last changes fastest.
Arguments:
- embeddings: bfloat16 [393216, 1024], P(('row', 'col')), may hold values from -40 to 40
- doc_ids: int32 [393216], P(('row', 'col')), may hold values from 0 to 393215, each once
- valid_counts: int32 [512], P(('row', 'col')), may hold values from 384 to 768
Outputs:
- nearest: float32 [393216], P(('row', 'col'))
The draws below stay inside these ranges and needn't reach their ends.
Inputs may be any that keep to these rules, and one draw needn't show every extreme that they name: `doc_ids`: the ids are distinct.
All inputs are finite; a program needn't handle non-finite values.
Results may differ from the reference program's by a relative error of at most 0.0005.
Values may be sent and summed in bfloat16 or wider, within the bound.
A program may use at most 64 MiB of HBM per device.

```python
import jax
import jax.numpy as jnp
from jax import lax

D = 1024
ROWS = 768
BAND = 4
BLOCKS = 512
DOCS = 393216


def draw_embeddings(key, part):
    base_key, offset_key, plant_key, strength_key = jax.random.split(jax.random.fold_in(key, 11), 4)
    base = jax.random.normal(base_key, (DOCS, D), jnp.float32)
    offsets = jax.random.randint(offset_key, (DOCS,), -(BAND * ROWS), BAND * ROWS + 1)
    source = jnp.clip(jnp.arange(DOCS, dtype=jnp.int32) + offsets, 0, DOCS - 1)
    planted = jax.random.uniform(plant_key, (DOCS,), jnp.float32) < 0.4
    strength = jax.random.uniform(strength_key, (DOCS,), jnp.float32, 0.5, 2.0)
    mixed = base + jnp.where(planted, strength, 0.0)[:, None] * base[source]
    return mixed.astype(jnp.bfloat16)


def touch_ends(array, rng, least, high):
    longest = array.shape.index(max(array.shape))
    spots = []
    for shift in (0, 1):
        where = [jax.random.randint(jax.random.fold_in(rng, axis), (), 0, length) for axis, length in enumerate(array.shape)]
        where[longest] = (where[longest] + shift) % array.shape[longest]
        spots.append(tuple(where))
    return array.at[spots[0]].set(least).at[spots[1]].set(high)


def setup_inputs(seed: int = 0) -> dict:
    arg_keys = jax.random.split(jax.random.key(seed), 4)
    return {
        "embeddings": draw_embeddings(jax.random.fold_in(arg_keys[3], 71), 0),
        "doc_ids": jax.random.permutation(arg_keys[1], DOCS).astype(jnp.int32),
        "valid_counts": touch_ends(jax.random.randint(arg_keys[2], (BLOCKS,), ROWS // 2, ROWS + 1), jax.random.fold_in(arg_keys[2], 1), ROWS // 2, ROWS).astype(jnp.int32),
    }


def normalize(embeddings):
    floats = embeddings.astype(jnp.float32)
    total = lax.optimization_barrier(jnp.sum(floats * floats, axis=-1, keepdims=True))
    return (floats * lax.rsqrt(total + 1e-06)).astype(jnp.bfloat16)

def pair_maxima(unit_left, ids_left, valid_left, unit_right, ids_right, valid_right):
    scores = lax.dot_general(unit_left, unit_right, (((1,), (1,)), ((), ())), preferred_element_type=jnp.float32)
    both = valid_left[:, None] & valid_right[None, :]
    lower = both & (ids_right[None, :] < ids_left[:, None])
    upper = both & (ids_left[:, None] < ids_right[None, :])
    row_best = lax.optimization_barrier(jnp.max(jnp.where(lower, scores, -1.0), axis=1))
    col_best = lax.optimization_barrier(jnp.max(jnp.where(upper, scores, -1.0), axis=0))
    return (row_best, col_best)

def reference(embeddings, doc_ids, valid_counts):
    block_count = valid_counts.shape[0]
    unit_all = normalize(embeddings).reshape(block_count, ROWS, -1)
    ids_all = doc_ids.reshape(block_count, ROWS)
    valid_all = lax.iota(jnp.int32, ROWS)[None, :] < valid_counts[:, None]

    def self_pair(index):
        row_best, col_best = pair_maxima(unit_all[index], ids_all[index], valid_all[index], unit_all[index], ids_all[index], valid_all[index])
        return row_best
    nearest = lax.map(self_pair, jnp.arange(block_count, dtype=jnp.int32))
    for shift_by in range(1, BAND + 1):

        def cross_pair(index):
            other = jnp.minimum(index + shift_by, block_count - 1).astype(jnp.int32)
            exists = index + shift_by < block_count
            return pair_maxima(unit_all[index], ids_all[index], valid_all[index], unit_all[other], ids_all[other], valid_all[other] & exists)
        row_best, col_best = lax.map(cross_pair, jnp.arange(block_count, dtype=jnp.int32))
        filler = jnp.full((shift_by, ROWS), -1.0, jnp.float32)
        col_back = jnp.concatenate([filler, col_best[:block_count - shift_by]], axis=0)
        nearest = jnp.maximum(nearest, jnp.maximum(row_best, col_back))
    return nearest.reshape(-1)
```

```python
import functools

import jax
import jax.numpy as jnp
from jax import lax
from jax.experimental import pallas as pl
from jax.experimental.pallas import tpu as pltpu
from jax.sharding import PartitionSpec as P

MESH = pl.DeviceIdType.MESH
FAR = 2**30
CHUNKS = 6
STEPS = 3
SLOTS = 5
LANES = 128

PAIRS = (
    (
        ((0, 0), (0, 2), (1, 2), (0, 1), (3, 0)),
        ((0, 0), (0, 2), (3, 0), (3, 1), (4, 1)),
        ((0, 0), (0, 2), (3, 0), (3, 1), (4, 1)),
        ((0, 0), (1, 2), (3, 0), (3, 1), (3, 2)),
    ),
    (
        ((0, 0), (0, 2), (1, 2), (3, 0), (4, 0)),
        ((0, 0), (0, 2), (3, 0), (4, 0), (4, 1)),
        ((0, 0), (0, 2), (3, 0), (4, 0), (4, 1)),
        ((0, 0), (0, 2), (1, 2), (3, 0), (3, 2)),
    ),
)


def host_of(block, planes, cols):
    row, col = block // cols, block % cols
    zlo, core = row // 2, row % 2
    plane = (zlo + planes // 2 + planes * ((zlo + core) % 2)) % (2 * planes)
    half = (col // 4) % 2
    return (plane % planes) * 2 + half, (col // 8) * 8 + (plane // planes) * 4 + col % 4


def kernel(
    rows, cols, emb_ref, ids_ref, count_ref, out_ref,
    own, blk, kown, kin, kcol, rowacc, colacc, rout, rin,
    zsend, bsend, fsend, recv, ksend, krecv, rsend, rrecv,
):
    planes, total = rows // 2, rows * cols
    size, depth = emb_ref.shape
    piece = size // CHUNKS
    row, col = lax.axis_index("row"), lax.axis_index("col")
    me = row * cols + col
    core, y, xi, half = row % 2, col % 4, col // 8, (col // 4) % 2
    level = (half * planes + row // 2 + 2 * planes - planes // 2) % (2 * planes)
    held_core = (level % planes + level // planes) % 2
    held = ((level % planes) * 2 + held_core) * cols + xi * 8 + core * 4 + y

    def host(block):
        return host_of(block, planes, cols)

    def home(block):
        return block // cols, block % cols

    has_next = me + 4 < total
    needed = (
        host(me),
        host(me - y + (y + 1) % 4),
        host(me - y + (y + 3) % 4),
        host(me + 4),
        host(me + 3),
    )
    needed_if = (None, None, None, has_next, has_next & (y >= 1 + half))
    homes = (
        home(held),
        home(held - y + (y + 3) % 4),
        home(held - y + (y + 1) % 4),
        home(held - 4),
        home(held - 3),
    )
    has_before = held >= 4
    homes_if = (None, None, None, has_before, has_before & (y <= 2) & (y >= 1 - core))
    crossing = (xi == cols // 8 - 1) & (half == 1) & (core == 0)
    up, down = host(held - y + (y + 1) % 4), host(held - y + (y + 3) % 4)
    after, before = host(held + 4), host(held - 4)
    has_after = held + 4 < total
    held_crossing = (core == 1) & (xi == cols // 8 - 1) & (held_core == 0)

    def when(condition, act):
        if condition is None:
            act()
        else:
            pl.when(condition)(act)

    barrier = pltpu.get_barrier_semaphore()

    def greet(device):
        pl.semaphore_signal(barrier, inc=1, device_id=device, device_id_type=MESH)

    for slot in range(SLOTS):
        when(needed_if[slot], functools.partial(greet, needed[slot]))
        when(homes_if[slot], functools.partial(greet, homes[slot]))
    greet(up)
    greet(down)
    when(has_after, functools.partial(greet, after))
    when(has_before, functools.partial(greet, before))

    def one(condition):
        return condition.astype(jnp.int32)

    greetings = (
        8
        + one(needed_if[3]) + one(needed_if[4]) + one(homes_if[3]) + one(homes_if[4])
        + one(has_after) + one(has_before)
    )

    places = lax.broadcasted_iota(jnp.int32, (1, size), 1)
    valid = places < count_ref[0]
    kown[...] = jnp.where(valid, ids_ref[...], FAR)
    rowacc[...] = jnp.full(rowacc.shape, -1.0, jnp.float32)
    colacc[...] = jnp.full(colacc.shape, -1.0, jnp.float32)
    pl.semaphore_wait(barrier, greetings)

    def key_copy(slot):
        return pltpu.make_async_remote_copy(
            src_ref=kown, dst_ref=kin.at[slot], send_sem=ksend.at[slot], recv_sem=krecv.at[slot],
            device_id=needed[slot], device_id_type=MESH,
        )

    def result_copy(slot):
        return pltpu.make_async_remote_copy(
            src_ref=rout.at[slot], dst_ref=rin.at[slot], send_sem=rsend.at[slot], recv_sem=rrecv.at[slot],
            device_id=homes[slot], device_id_type=MESH,
        )

    def part(c):
        return pl.ds(pl.multiple_of(c * piece, piece), piece)

    def first_copy(c, slot, sems):
        return pltpu.make_async_remote_copy(
            src_ref=own.at[part(c)], dst_ref=blk.at[slot, part(c)], send_sem=sems.at[c],
            recv_sem=recv.at[slot, c], device_id=needed[slot], device_id_type=MESH,
        )

    def forward(c, way, source, target, device):
        return pltpu.make_async_remote_copy(
            src_ref=blk.at[source, part(c)], dst_ref=blk.at[target, part(c)], send_sem=fsend.at[way, c],
            recv_sem=recv.at[target, c], device_id=device, device_id_type=MESH,
        )

    forwards = (
        (0, 0, 1, up, None),
        (1, 0, 2, down, None),
        (2, 0, 3, after, has_after & jnp.logical_not(held_crossing)),
        (3, 2, 4, after, (core == 0) & (y <= 2)),
        (4, 3, 4, down, (core == 0) & (y >= 2) & has_before),
    )

    for slot in range(SLOTS):
        when(needed_if[slot], lambda slot=slot: key_copy(slot).start())

    @pl.loop(0, CHUNKS)
    def _(c):
        floats = emb_ref[part(c), :].astype(jnp.float32)
        sums = jnp.sum(floats * floats, axis=-1, keepdims=True)
        own[part(c), :] = (floats * lax.rsqrt(sums + 1e-06)).astype(jnp.bfloat16)
        first_copy(c, 0, zsend).start()
        pl.when(crossing)(lambda: first_copy(c, 3, bsend).start())

    for slot in range(SLOTS):

        @functools.partial(when, homes_if[slot])
        def _(slot=slot):
            key_copy(slot).wait_recv()
            for g in range(size // LANES):
                lanes = slice(g * LANES, (g + 1) * LANES)
                kcol[slot, lanes, :] = jnp.broadcast_to(kin[slot, :, lanes], (LANES, LANES)).T

    lefts, rights = [], []
    for p in range(SLOTS):
        for side, kept in ((0, lefts), (1, rights)):
            value = jnp.int32(PAIRS[0][0][p][side])
            for k in range(2):
                for j in range(4):
                    other = PAIRS[k][j][p][side]
                    value = jnp.where((core == k) & (y == j), other, value)
            kept.append(value)
    skipped = jnp.where(y == 0, 1, 3)
    pairs = jnp.where(has_before, SLOTS, SLOTS - skipped)

    def pick(values, p):
        value = values[0]
        for k in range(1, SLOTS):
            value = jnp.where(p == k, values[k], value)
        return value

    def tile(left, right, i, count, j, width):
        scores = lax.dot_general(
            blk[left, i : i + count, :], blk[right, j : j + width, :],
            (((1,), (1,)), ((), ())), preferred_element_type=jnp.float32,
        )
        mine = kcol[left, i : i + count, :]
        best = rowacc[left, i : i + count, :]
        for g in range(width // LANES):
            lanes = slice(j + g * LANES, j + (g + 1) * LANES)
            part_scores = scores[:, g * LANES : (g + 1) * LANES]
            theirs = kin[right, :, lanes]
            best = jnp.maximum(best, jnp.where(theirs < mine, part_scores, -1.0))
            upper = jnp.where(mine < theirs, part_scores, -1.0)
            upper = jnp.max(upper.reshape(count // 8, 8, LANES), axis=0)
            colacc[right, :, lanes] = jnp.maximum(colacc[right, :, lanes], upper)
        rowacc[left, i : i + count, :] = best

    step = size // STEPS
    for k in range(STEPS):

        @pl.loop(k * CHUNKS // STEPS, (k + 1) * CHUNKS // STEPS)
        def _(c):
            for slot in range(SLOTS):

                @functools.partial(when, homes_if[slot])
                def _(slot=slot):
                    forward(c, 0, slot, slot, up).wait_recv()

                for way, source, target, device, condition in forwards:
                    if source == slot:
                        when(condition, lambda: forward(c, way, source, target, device).start())

        @pl.loop(0, pairs)
        def _(p):
            left, right = pick(lefts, p), pick(rights, p)
            tile(left, right, k * step, step, 0, (k + 1) * step)
            for i in range(k):
                tile(left, right, i * step, step, k * step, step)

    for slot in (3, 4, 1, 2, 0):

        @functools.partial(when, homes_if[slot])
        def _(slot=slot):
            best = jnp.max(colacc[slot], axis=0, keepdims=True)
            for g in range(size // LANES):
                lanes = slice(g * LANES, (g + 1) * LANES)
                across = jnp.max(rowacc[slot, lanes, :].T, axis=0, keepdims=True)
                rout[slot, :, lanes] = jnp.maximum(best[:, lanes], across)
            result_copy(slot).start()

    @pl.loop(0, CHUNKS)
    def _(c):
        first_copy(c, 0, zsend).wait_send()
        pl.when(crossing)(lambda: first_copy(c, 3, bsend).wait_send())
        for way, source, target, device, condition in forwards:
            when(condition, lambda: forward(c, way, source, target, device).wait_send())

    for slot in range(SLOTS):
        when(needed_if[slot], lambda slot=slot: key_copy(slot).wait_send())

    for slot in range(SLOTS):

        @functools.partial(when, needed_if[slot])
        def _(slot=slot):
            result_copy(slot).wait_recv()
            if slot == 0:
                out_ref[...] = rin[slot]
            else:
                out_ref[...] = jnp.maximum(out_ref[...], rin[slot])

    out_ref[...] = jnp.where(valid, out_ref[...], -1.0)
    for slot in range(SLOTS):
        when(homes_if[slot], lambda slot=slot: result_copy(slot).wait_send())


def solution(mesh):
    rows, cols = mesh.shape["row"], mesh.shape["col"]

    def local(embeddings, doc_ids, valid_counts):
        size, depth = embeddings.shape
        vmem = pl.BlockSpec(memory_space=pltpu.VMEM)
        nearest = pl.pallas_call(
            functools.partial(kernel, rows, cols),
            out_shape=jax.ShapeDtypeStruct((1, size), jnp.float32),
            in_specs=[vmem, vmem, pl.BlockSpec(memory_space=pltpu.SMEM)],
            out_specs=vmem,
            scratch_shapes=[
                pltpu.VMEM((size, depth), jnp.bfloat16),
                pltpu.VMEM((SLOTS, size, depth), jnp.bfloat16),
                pltpu.VMEM((1, size), jnp.int32),
                pltpu.VMEM((SLOTS, 1, size), jnp.int32),
                pltpu.VMEM((SLOTS, size, LANES), jnp.int32),
                pltpu.VMEM((SLOTS, size, LANES), jnp.float32),
                pltpu.VMEM((SLOTS, 8, size), jnp.float32),
                pltpu.VMEM((SLOTS, 1, size), jnp.float32),
                pltpu.VMEM((SLOTS, 1, size), jnp.float32),
                pltpu.SemaphoreType.DMA((CHUNKS,)),
                pltpu.SemaphoreType.DMA((CHUNKS,)),
                pltpu.SemaphoreType.DMA((SLOTS, CHUNKS)),
                pltpu.SemaphoreType.DMA((SLOTS, CHUNKS)),
                pltpu.SemaphoreType.DMA((SLOTS,)),
                pltpu.SemaphoreType.DMA((SLOTS,)),
                pltpu.SemaphoreType.DMA((SLOTS,)),
                pltpu.SemaphoreType.DMA((SLOTS,)),
            ],
            compiler_params=pltpu.CompilerParams(
                collective_id=0, has_side_effects=True, vmem_limit_bytes=48 * 2**20
            ),
            cost_estimate=pl.CostEstimate(
                flops=10 * size * size * depth, bytes_accessed=4 * size * depth, transcendentals=0
            ),
        )(embeddings, doc_ids.reshape(1, size), valid_counts)
        return nearest.reshape(size)

    in_specs = (P(("row", "col"), None), P(("row", "col")), P(("row", "col")))
    return jax.shard_map(
        local, mesh=mesh, in_specs=in_specs, out_specs=P(("row", "col")), check_vma=False
    )
```

```python
import functools

import jax
import jax.numpy as jnp
from jax import lax
from jax.experimental import pallas as pl
from jax.experimental.pallas import tpu as pltpu
from jax.sharding import PartitionSpec as P

MESH = pl.DeviceIdType.MESH
FAR = 2**30
CHUNKS = 8
STEPS = 3
SLOTS = 5
LANES = 128

PAIRS = (
    (
        ((0, 0), (0, 2), (0, 1), (3, 0), (4, 2)),
        ((0, 0), (0, 2), (1, 2), (3, 0), (3, 1)),
        ((0, 0), (0, 2), (1, 2), (3, 0), (3, 1)),
        ((0, 0), (3, 0), (3, 1), (3, 2), (4, 2)),
    ),
    (
        ((0, 0), (0, 2), (1, 2), (0, 1), (3, 0)),
        ((0, 0), (0, 2), (3, 0), (3, 1), (4, 1)),
        ((0, 0), (0, 2), (3, 0), (3, 1), (4, 1)),
        ((0, 0), (1, 2), (3, 0), (3, 1), (3, 2)),
    ),
)
AHEAD = 3


def host_of(block, planes, cols):
    row, col = block // cols, block % cols
    zlo, core = row // 2, row % 2
    plane = (zlo + planes // 2 + planes * ((zlo + core) % 2)) % (2 * planes)
    half = (col // 4) % 2
    return (plane % planes) * 2 + half, (col // 8) * 8 + (plane // planes) * 4 + col % 4


def kernel(
    rows, cols, emb_ref, ids_ref, count_ref, out_ref,
    own, relayed, blk, kown, kin, kcol, rowacc, colacc, rout, rin,
    zsend, bsend, msend, mrecv, fsend, recv, ksend, krecv, rsend, rrecv,
):
    planes, total = rows // 2, rows * cols
    size, depth = emb_ref.shape
    piece = size // CHUNKS
    row, col = lax.axis_index("row"), lax.axis_index("col")
    me = row * cols + col
    core, y, xi, half = row % 2, col % 4, col // 8, (col // 4) % 2
    level = (half * planes + row // 2 + 2 * planes - planes // 2) % (2 * planes)
    held_core = (level % planes + level // planes) % 2
    held = ((level % planes) * 2 + held_core) * cols + xi * 8 + core * 4 + y

    def host(block):
        return host_of(block, planes, cols)

    def home(block):
        return block // cols, block % cols

    has_next = me + 4 < total
    needed = (
        host(me),
        host(me - y + (y + 1) % 4),
        host(me - y + (y + 3) % 4),
        host(me + 4),
        host(me + 4 - half * (y - (y + 1) % 4) - (1 - half)),
    )
    needed_if = (None, None, None, has_next, has_next & (y >= 2))
    homes = (
        home(held),
        home(held - y + (y + 3) % 4),
        home(held - y + (y + 1) % 4),
        home(held - 4),
        home(held - 4 + core - (1 - core) * (y - (y + 3) % 4)),
    )
    has_before = held >= 4
    far_in = jnp.where(core == 0, (y == 0) | (y == 3), (y == 1) | (y == 2))
    homes_if = (None, None, None, has_before, has_before & far_in)
    routes = cols // 8
    last = routes - 1
    crossing = (xi == last) & (half == 1) & (core == 0)
    leaving = (xi == last) & (core == 1) & (held_core == 1) & (held + 4 < total)
    relay_first = (xi < last) & (half == 1) & (core == 0)
    relay_next = held + (last - xi) * 8 + 4
    relay_later = (xi < last) & (core == 1) & (held_core == 1) & (relay_next < total)
    relay = relay_first | relay_later
    relay_to = host(jnp.where(core == 0, me + (last - xi) * 8 + 4, relay_next))
    entering = (core == 0) & (xi == 0) & has_before
    up, down = host(held - y + (y + 1) % 4), host(held - y + (y + 3) % 4)
    after, before = host(held + 4), host(held - 4)
    far = host(held + 4 - core * (y - (y + 1) % 4) - (1 - core))
    has_after = held + 4 < total
    passes = has_after & jnp.logical_not((core == 1) & (xi == last))

    def when(condition, act):
        if condition is None:
            act()
        else:
            pl.when(condition)(act)

    def one_if(condition):
        return condition.astype(jnp.int32)

    barrier = pltpu.get_barrier_semaphore()

    def greet(device):
        pl.semaphore_signal(barrier, inc=1, device_id=device, device_id_type=MESH)

    for slot in range(SLOTS):
        when(needed_if[slot], functools.partial(greet, needed[slot]))
        when(homes_if[slot], functools.partial(greet, homes[slot]))
    greet(up)
    greet(down)
    when(has_after, functools.partial(greet, after))
    when(has_before, functools.partial(greet, before))
    greet_far_from = host(held - 4 + core - (1 - core) * (y - (y + 3) % 4))
    when(passes & (y >= 2), functools.partial(greet, far))
    far_from = homes_if[4] & jnp.logical_not(entering)
    when(far_from, functools.partial(greet, greet_far_from))

    def lane(k):
        return row, col - (xi - k) * 8

    for k in range(last):
        when(crossing | leaving, functools.partial(greet, lane(k)))
    when(relay, functools.partial(greet, lane(last)))
    when(relay, functools.partial(greet, relay_to))
    entry_row = jnp.where(held_core == 1, homes[3][0], before[0])
    entry_col = jnp.where(held_core == 1, homes[3][1], before[1])
    for k in range(last):
        when(entering, functools.partial(greet, (entry_row, entry_col - (last - k) * 8)))

    greetings = (
        8
        + one_if(needed_if[3]) + one_if(needed_if[4]) + one_if(homes_if[3]) + one_if(homes_if[4])
        + one_if(has_after) + one_if(has_before) + one_if(passes & (y >= 2)) + one_if(far_from)
        + last * one_if(crossing | leaving) + 2 * one_if(relay) + last * one_if(entering)
    )

    places = lax.broadcasted_iota(jnp.int32, (1, size), 1)
    valid = places < count_ref[0]
    kown[...] = jnp.where(valid, ids_ref[...], FAR)
    rowacc[...] = jnp.full(rowacc.shape, -1.0, jnp.float32)
    colacc[...] = jnp.full(colacc.shape, -1.0, jnp.float32)
    pl.semaphore_wait(barrier, greetings)

    def key_copy(slot):
        return pltpu.make_async_remote_copy(
            src_ref=kown, dst_ref=kin.at[slot], send_sem=ksend.at[slot], recv_sem=krecv.at[slot],
            device_id=needed[slot], device_id_type=MESH,
        )

    def result_copy(slot):
        return pltpu.make_async_remote_copy(
            src_ref=rout.at[slot], dst_ref=rin.at[slot], send_sem=rsend.at[slot], recv_sem=rrecv.at[slot],
            device_id=homes[slot], device_id_type=MESH,
        )

    def part(c):
        return pl.ds(pl.multiple_of(c * piece, piece), piece)

    def first_copy(c, slot, sems):
        return pltpu.make_async_remote_copy(
            src_ref=own.at[part(c)], dst_ref=blk.at[slot, part(c)], send_sem=sems.at[c],
            recv_sem=recv.at[slot, c], device_id=needed[slot], device_id_type=MESH,
        )

    def forward(c, way, source, target, device):
        return pltpu.make_async_remote_copy(
            src_ref=blk.at[source, part(c)], dst_ref=blk.at[target, part(c)], send_sem=fsend.at[way, c],
            recv_sem=recv.at[target, c], device_id=device, device_id_type=MESH,
        )

    forwards = (
        (0, 0, 1, up, None),
        (1, 0, 2, down, None),
        (2, 0, 3, after, passes),
        (3, 0, 4, far, passes & (y >= 2)),
    )
    entered = (4, 3, 4, up)
    entered_on = entering & (y >= 2)

    def relay_in(c, source):
        k, turn = c % routes, c // routes
        return pltpu.make_async_remote_copy(
            src_ref=source.at[part(c)], dst_ref=relayed.at[turn], send_sem=bsend.at[c],
            recv_sem=mrecv.at[turn], device_id=(row, col - (xi - k) * 8), device_id_type=MESH,
        )

    def relay_out(turn):
        c = turn * routes + xi
        return pltpu.make_async_remote_copy(
            src_ref=relayed.at[turn], dst_ref=blk.at[3, part(c)], send_sem=msend.at[turn],
            recv_sem=recv.at[3, c], device_id=relay_to, device_id_type=MESH,
        )

    for slot in range(SLOTS):
        when(needed_if[slot], lambda slot=slot: key_copy(slot).start())

    @pl.loop(0, CHUNKS)
    def _(c):
        floats = emb_ref[part(c), :].astype(jnp.float32)
        sums = jnp.sum(floats * floats, axis=-1, keepdims=True)
        own[part(c), :] = (floats * lax.rsqrt(sums + 1e-06)).astype(jnp.bfloat16)
        pl.when(c < 2)(lambda: first_copy(c, 0, zsend).start())
        pl.when(crossing & (c % routes == last))(lambda: first_copy(c, 3, bsend).start())
        pl.when(crossing & (c % routes != last))(lambda: relay_in(c, own).start())

    for slot in range(SLOTS):

        @functools.partial(when, homes_if[slot])
        def _(slot=slot):
            key_copy(slot).wait_recv()
            for g in range(size // LANES):
                lanes = slice(g * LANES, (g + 1) * LANES)
                kcol[slot, lanes, :] = jnp.broadcast_to(kin[slot, :, lanes], (LANES, LANES)).T

    for turn in range(CHUNKS // routes):

        @pl.when(relay_first)
        def _(turn=turn):
            relay_in(turn * routes, own).wait_recv()
            relay_out(turn).start()

    lefts, rights = [], []
    for p in range(SLOTS):
        for side, kept in ((0, lefts), (1, rights)):
            value = jnp.int32(PAIRS[0][0][p][side])
            for k in range(2):
                for j in range(4):
                    other = PAIRS[k][j][p][side]
                    value = jnp.where((core == k) & (y == j), other, value)
            kept.append(value)
    skipped = jnp.where(y == 3, 4, 2)
    pairs = jnp.where(has_before, SLOTS, SLOTS - skipped)

    def pick(values, p):
        value = values[0]
        for k in range(1, SLOTS):
            value = jnp.where(p == k, values[k], value)
        return value

    def tile(left, right, i, count, j, width):
        scores = lax.dot_general(
            blk[left, i : i + count, :], blk[right, j : j + width, :],
            (((1,), (1,)), ((), ())), preferred_element_type=jnp.float32,
        )
        mine = kcol[left, i : i + count, :]
        best = rowacc[left, i : i + count, :]
        for g in range(width // LANES):
            lanes = slice(j + g * LANES, j + (g + 1) * LANES)
            part_scores = scores[:, g * LANES : (g + 1) * LANES]
            theirs = kin[right, :, lanes]
            best = jnp.maximum(best, jnp.where(theirs < mine, part_scores, -1.0))
            upper = jnp.where(mine < theirs, part_scores, -1.0)
            upper = jnp.max(upper.reshape(count // 8, 8, LANES), axis=0)
            colacc[right, :, lanes] = jnp.maximum(colacc[right, :, lanes], upper)
        rowacc[left, i : i + count, :] = best

    step = size // STEPS

    def advance(c):
        forward(c, 0, 0, 0, up).wait_recv()
        for way, source, target, device, condition in forwards:
            when(condition, lambda: forward(c, way, source, target, device).start())
        pl.when(leaving & (c % routes == last))(lambda: forward(c, 2, 0, 3, after).start())
        pl.when(leaving & (c % routes != last))(lambda: relay_in(c, blk.at[0]).start())

    def pass_on(c):
        @pl.when(relay_later & (c % routes == xi))
        def _():
            relay_in(c, own).wait_recv()
            relay_out(c // routes).start()

    def enter(c):
        @pl.when(entered_on)
        def _():
            forward(c, 0, 3, 3, up).wait_recv()
            forward(c, *entered).start()

    def arrive(c):
        for slot in range(1, SLOTS):
            condition = homes_if[slot]
            if slot == 3:
                condition = condition & jnp.logical_not(entered_on)
            when(condition, lambda: forward(c, 0, slot, slot, up).wait_recv())

    need = [-(-(k + 1) * step // piece) for k in range(STEPS)]
    ahead = [min(n + AHEAD, CHUNKS + 2) for n in need[:-1]] + [CHUNKS + 2]
    for k in range(STEPS):

        @pl.loop(ahead[k - 1] if k else 0, ahead[k])
        def _(i):
            pl.when(i < CHUNKS)(lambda: advance(i))
            pl.when(i + 2 < CHUNKS)(lambda: first_copy(i + 2, 0, zsend).start())
            pl.when((i >= 1) & (i <= CHUNKS))(lambda: pass_on(i - 1))
            pl.when(i >= 2)(lambda: enter(i - 2))

        pl.loop(need[k - 1] if k else 0, need[k])(arrive)

        @pl.loop(0, pairs)
        def _(p):
            left, right = pick(lefts, p), pick(rights, p)
            tile(left, right, k * step, step, 0, (k + 1) * step)
            for i in range(k):
                tile(left, right, i * step, step, k * step, step)

    for slot in (3, 4, 1, 2, 0):

        @functools.partial(when, homes_if[slot])
        def _(slot=slot):
            if slot < 3:
                best = jnp.max(colacc[slot], axis=0, keepdims=True)
            for g in range(size // LANES):
                lanes = slice(g * LANES, (g + 1) * LANES)
                if slot != 2:
                    across = jnp.max(rowacc[slot, lanes, :].T, axis=0, keepdims=True)
                if slot > 2:
                    rout[slot, :, lanes] = across
                elif slot == 2:
                    rout[slot, :, lanes] = best[:, lanes]
                else:
                    rout[slot, :, lanes] = jnp.maximum(best[:, lanes], across)
            result_copy(slot).start()

    @pl.loop(0, CHUNKS)
    def _(c):
        first_copy(c, 0, zsend).wait_send()
        pl.when(crossing & (c % routes == last))(lambda: first_copy(c, 3, bsend).wait_send())
        pl.when(crossing & (c % routes != last))(lambda: relay_in(c, own).wait_send())
        pl.when(leaving & (c % routes == last))(lambda: forward(c, 2, 0, 3, after).wait_send())
        pl.when(leaving & (c % routes != last))(lambda: relay_in(c, blk.at[0]).wait_send())
        pl.when(entered_on)(lambda: forward(c, *entered).wait_send())
        for way, source, target, device, condition in forwards:
            when(condition, lambda: forward(c, way, source, target, device).wait_send())

    for turn in range(CHUNKS // routes):
        pl.when(relay)(lambda turn=turn: relay_out(turn).wait_send())
    for slot in range(SLOTS):
        when(needed_if[slot], lambda slot=slot: key_copy(slot).wait_send())

    for slot in range(SLOTS):

        @functools.partial(when, needed_if[slot])
        def _(slot=slot):
            result_copy(slot).wait_recv()
            if slot == 0:
                out_ref[...] = rin[slot]
            else:
                out_ref[...] = jnp.maximum(out_ref[...], rin[slot])

    out_ref[...] = jnp.where(valid, out_ref[...], -1.0)
    for slot in range(SLOTS):
        when(homes_if[slot], lambda slot=slot: result_copy(slot).wait_send())


def solution(mesh):
    rows, cols = mesh.shape["row"], mesh.shape["col"]
    routes = cols // 8

    def local(embeddings, doc_ids, valid_counts):
        size, depth = embeddings.shape
        vmem = pl.BlockSpec(memory_space=pltpu.VMEM)
        nearest = pl.pallas_call(
            functools.partial(kernel, rows, cols),
            out_shape=jax.ShapeDtypeStruct((1, size), jnp.float32),
            in_specs=[vmem, vmem, pl.BlockSpec(memory_space=pltpu.SMEM)],
            out_specs=vmem,
            scratch_shapes=[
                pltpu.VMEM((size, depth), jnp.bfloat16),
                pltpu.VMEM((CHUNKS // routes, size // CHUNKS, depth), jnp.bfloat16),
                pltpu.VMEM((SLOTS, size, depth), jnp.bfloat16),
                pltpu.VMEM((1, size), jnp.int32),
                pltpu.VMEM((SLOTS, 1, size), jnp.int32),
                pltpu.VMEM((SLOTS, size, LANES), jnp.int32),
                pltpu.VMEM((SLOTS, size, LANES), jnp.float32),
                pltpu.VMEM((SLOTS, 8, size), jnp.float32),
                pltpu.VMEM((SLOTS, 1, size), jnp.float32),
                pltpu.VMEM((SLOTS, 1, size), jnp.float32),
                pltpu.SemaphoreType.DMA((CHUNKS,)),
                pltpu.SemaphoreType.DMA((CHUNKS,)),
                pltpu.SemaphoreType.DMA((CHUNKS // routes,)),
                pltpu.SemaphoreType.DMA((CHUNKS // routes,)),
                pltpu.SemaphoreType.DMA((SLOTS, CHUNKS)),
                pltpu.SemaphoreType.DMA((SLOTS, CHUNKS)),
                pltpu.SemaphoreType.DMA((SLOTS,)),
                pltpu.SemaphoreType.DMA((SLOTS,)),
                pltpu.SemaphoreType.DMA((SLOTS,)),
                pltpu.SemaphoreType.DMA((SLOTS,)),
            ],
            compiler_params=pltpu.CompilerParams(
                collective_id=0, has_side_effects=True, vmem_limit_bytes=48 * 2**20
            ),
            cost_estimate=pl.CostEstimate(
                flops=10 * size * size * depth, bytes_accessed=4 * size * depth, transcendentals=0
            ),
        )(embeddings, doc_ids.reshape(1, size), valid_counts)
        return nearest.reshape(size)

    in_specs = (P(("row", "col"), None), P(("row", "col")), P(("row", "col")))
    return jax.shard_map(
        local, mesh=mesh, in_specs=in_specs, out_specs=P(("row", "col")), check_vma=False
    )
```

```python
import functools

import jax
import jax.numpy as jnp
from jax import lax
from jax.experimental import pallas as pl
from jax.experimental.pallas import tpu as pltpu
from jax.sharding import PartitionSpec as P

MESH = pl.DeviceIdType.MESH
FAR = 2**30
CHUNKS = 12
STEPS = 3
SLOTS = 5
LANES = 128

PAIRS = (
    (
        ((0, 0), (0, 2), (0, 1), (3, 0), (4, 2)),
        ((0, 0), (0, 2), (1, 2), (3, 0), (3, 1)),
        ((0, 0), (0, 2), (1, 2), (3, 0), (3, 1)),
        ((0, 0), (3, 0), (3, 1), (3, 2), (4, 2)),
    ),
    (
        ((0, 0), (0, 2), (1, 2), (0, 1), (3, 0)),
        ((0, 0), (0, 2), (3, 0), (3, 1), (4, 1)),
        ((0, 0), (0, 2), (3, 0), (3, 1), (4, 1)),
        ((0, 0), (1, 2), (3, 0), (3, 1), (3, 2)),
    ),
)
FLYING = 3


def host_of(block, planes, cols):
    row, col = block // cols, block % cols
    zlo, core = row // 2, row % 2
    plane = (zlo + planes // 2 + planes * ((zlo + core) % 2)) % (2 * planes)
    half = (col // 4) % 2
    return (plane % planes) * 2 + half, (col // 8) * 8 + (plane // planes) * 4 + col % 4


def kernel(
    rows, cols, emb_hbm, ids_ref, count_ref, out_ref,
    emb_ref, esem, own, relayed, blk, kown, kin, kcol, rowacc, colacc, rout, rin,
    zsend, bsend, msend, mrecv, fsend, recv, ksend, krecv, rsend, rrecv,
):
    planes, total = rows // 2, rows * cols
    size, depth = emb_hbm.shape
    piece = size // CHUNKS
    row, col = lax.axis_index("row"), lax.axis_index("col")
    me = row * cols + col
    core, y, xi, half = row % 2, col % 4, col // 8, (col // 4) % 2
    level = (half * planes + row // 2 + 2 * planes - planes // 2) % (2 * planes)
    held_core = (level % planes + level // planes) % 2
    held = ((level % planes) * 2 + held_core) * cols + xi * 8 + core * 4 + y

    def host(block):
        return host_of(block, planes, cols)

    def home(block):
        return block // cols, block % cols

    has_next = me + 4 < total
    needed = (
        host(me),
        host(me - y + (y + 1) % 4),
        host(me - y + (y + 3) % 4),
        host(me + 4),
        host(me + 4 - half * (y - (y + 1) % 4) - (1 - half)),
    )
    needed_if = (None, None, None, has_next, has_next & (y >= 2))
    homes = (
        home(held),
        home(held - y + (y + 3) % 4),
        home(held - y + (y + 1) % 4),
        home(held - 4),
        home(held - 4 + core - (1 - core) * (y - (y + 3) % 4)),
    )
    has_before = held >= 4
    far_in = jnp.where(core == 0, (y == 0) | (y == 3), (y == 1) | (y == 2))
    homes_if = (None, None, None, has_before, has_before & far_in)
    routes = cols // 8
    last = routes - 1
    crossing = (xi == last) & (half == 1) & (core == 0)
    leaving = (xi == last) & (core == 1) & (held_core == 1) & (held + 4 < total)
    relay_first = (xi < last) & (half == 1) & (core == 0)
    relay_next = held + (last - xi) * 8 + 4
    relay_later = (xi < last) & (core == 1) & (held_core == 1) & (relay_next < total)
    relay = relay_first | relay_later
    relay_to = host(jnp.where(core == 0, me + (last - xi) * 8 + 4, relay_next))
    entering = (core == 0) & (xi == 0) & has_before
    up, down = host(held - y + (y + 1) % 4), host(held - y + (y + 3) % 4)
    after, before = host(held + 4), host(held - 4)
    far = host(held + 4 - core * (y - (y + 1) % 4) - (1 - core))
    has_after = held + 4 < total
    passes = has_after & jnp.logical_not((core == 1) & (xi == last))

    def when(condition, act):
        if condition is None:
            act()
        else:
            pl.when(condition)(act)

    def one_if(condition):
        return condition.astype(jnp.int32)

    barrier = pltpu.get_barrier_semaphore()

    def part(c):
        return pl.ds(pl.multiple_of(c * piece, piece), piece)

    def load(c):
        return pltpu.make_async_copy(emb_hbm.at[part(c)], emb_ref.at[part(c)], esem.at[c])


    def greet(device):
        pl.semaphore_signal(barrier, inc=1, device_id=device, device_id_type=MESH)

    for slot in range(SLOTS):
        when(needed_if[slot], functools.partial(greet, needed[slot]))
        when(homes_if[slot], functools.partial(greet, homes[slot]))
    greet(up)
    greet(down)
    when(has_after, functools.partial(greet, after))
    when(has_before, functools.partial(greet, before))
    greet_far_from = host(held - 4 + core - (1 - core) * (y - (y + 3) % 4))
    when(passes & (y >= 2), functools.partial(greet, far))
    far_from = homes_if[4] & jnp.logical_not(entering)
    when(far_from, functools.partial(greet, greet_far_from))

    def lane(k):
        return row, col - (xi - k) * 8

    for k in range(last):
        when(crossing | leaving, functools.partial(greet, lane(k)))
    when(relay, functools.partial(greet, lane(last)))
    when(relay, functools.partial(greet, relay_to))
    entry_row = jnp.where(held_core == 1, homes[3][0], before[0])
    entry_col = jnp.where(held_core == 1, homes[3][1], before[1])
    for k in range(last):
        when(entering, functools.partial(greet, (entry_row, entry_col - (last - k) * 8)))

    greetings = (
        8
        + one_if(needed_if[3]) + one_if(needed_if[4]) + one_if(homes_if[3]) + one_if(homes_if[4])
        + one_if(has_after) + one_if(has_before) + one_if(passes & (y >= 2)) + one_if(far_from)
        + last * one_if(crossing | leaving) + 2 * one_if(relay) + last * one_if(entering)
    )

    pl.loop(0, CHUNKS)(lambda c: load(c).start())
    places = lax.broadcasted_iota(jnp.int32, (1, size), 1)
    valid = places < count_ref[0]
    kown[...] = jnp.where(valid, ids_ref[...].reshape(1, size), FAR)
    rowacc[...] = jnp.full(rowacc.shape, -1.0, jnp.float32)
    colacc[...] = jnp.full(colacc.shape, -1.0, jnp.float32)
    pl.semaphore_wait(barrier, greetings)

    def key_copy(slot):
        return pltpu.make_async_remote_copy(
            src_ref=kown, dst_ref=kin.at[slot], send_sem=ksend.at[slot], recv_sem=krecv.at[slot],
            device_id=needed[slot], device_id_type=MESH,
        )

    def result_copy(slot):
        return pltpu.make_async_remote_copy(
            src_ref=rout.at[slot], dst_ref=rin.at[slot], send_sem=rsend.at[slot], recv_sem=rrecv.at[slot],
            device_id=homes[slot], device_id_type=MESH,
        )

    def first_copy(c, slot, sems):
        return pltpu.make_async_remote_copy(
            src_ref=own.at[part(c)], dst_ref=blk.at[slot, part(c)], send_sem=sems.at[c],
            recv_sem=recv.at[slot, c], device_id=needed[slot], device_id_type=MESH,
        )

    def forward(c, way, source, target, device):
        return pltpu.make_async_remote_copy(
            src_ref=blk.at[source, part(c)], dst_ref=blk.at[target, part(c)], send_sem=fsend.at[way, c],
            recv_sem=recv.at[target, c], device_id=device, device_id_type=MESH,
        )

    forwards = (
        (0, 0, 1, up, None),
        (1, 0, 2, down, None),
        (2, 0, 3, after, passes),
        (3, 0, 4, far, passes & (y >= 2)),
    )
    entered = (4, 3, 4, up)
    entered_on = entering & (y >= 2)

    def relay_in(c, source):
        k, turn = c % routes, c // routes
        return pltpu.make_async_remote_copy(
            src_ref=source.at[part(c)], dst_ref=relayed.at[turn], send_sem=bsend.at[c],
            recv_sem=mrecv.at[turn], device_id=(row, col - (xi - k) * 8), device_id_type=MESH,
        )

    def relay_out(turn):
        c = turn * routes + xi
        return pltpu.make_async_remote_copy(
            src_ref=relayed.at[turn], dst_ref=blk.at[3, part(c)], send_sem=msend.at[turn],
            recv_sem=recv.at[3, c], device_id=relay_to, device_id_type=MESH,
        )

    for slot in range(SLOTS):
        when(needed_if[slot], lambda slot=slot: key_copy(slot).start())

    @pl.loop(0, CHUNKS)
    def _(c):
        load(c).wait()
        floats = emb_ref[part(c), :].astype(jnp.float32)
        sums = jnp.sum(floats * floats, axis=-1, keepdims=True)
        own[part(c), :] = (floats * lax.rsqrt(sums + 1e-06)).astype(jnp.bfloat16)
        pl.when(c < FLYING)(lambda: first_copy(c, 0, zsend).start())
        pl.when(crossing & (c % routes == last))(lambda: first_copy(c, 3, bsend).start())
        pl.when(crossing & (c % routes != last))(lambda: relay_in(c, own).start())

    for slot in range(SLOTS):

        @functools.partial(when, homes_if[slot])
        def _(slot=slot):
            key_copy(slot).wait_recv()
            for g in range(size // LANES):
                lanes = slice(g * LANES, (g + 1) * LANES)
                kcol[slot, lanes, :] = jnp.broadcast_to(kin[slot, :, lanes], (LANES, LANES)).T

    for turn in range(CHUNKS // routes):

        @pl.when(relay_first)
        def _(turn=turn):
            relay_in(turn * routes, own).wait_recv()
            relay_out(turn).start()

    lefts, rights = [], []
    for p in range(SLOTS):
        for side, kept in ((0, lefts), (1, rights)):
            value = jnp.int32(PAIRS[0][0][p][side])
            for k in range(2):
                for j in range(4):
                    other = PAIRS[k][j][p][side]
                    value = jnp.where((core == k) & (y == j), other, value)
            kept.append(value)
    inner = jnp.where(core == 0, jnp.where(y == 3, 1, 3), jnp.where(y == 0, 4, 2))
    pairs = jnp.where(has_before, SLOTS, inner)

    def pick(values, p):
        value = values[0]
        for k in range(1, SLOTS):
            value = jnp.where(p == k, values[k], value)
        return value

    def tile(left, right, i, count, j, width):
        scores = lax.dot_general(
            blk[left, i : i + count, :], blk[right, j : j + width, :],
            (((1,), (1,)), ((), ())), preferred_element_type=jnp.float32,
        )
        mine = kcol[left, i : i + count, :]
        best = rowacc[left, i : i + count, :]
        for g in range(width // LANES):
            lanes = slice(j + g * LANES, j + (g + 1) * LANES)
            part_scores = scores[:, g * LANES : (g + 1) * LANES]
            theirs = kin[right, :, lanes]
            best = jnp.maximum(best, jnp.where(theirs < mine, part_scores, -1.0))
            upper = jnp.where(mine < theirs, part_scores, -1.0)
            upper = jnp.max(upper.reshape(count // 8, 8, LANES), axis=0)
            colacc[right, :, lanes] = jnp.maximum(colacc[right, :, lanes], upper)
        rowacc[left, i : i + count, :] = best

    step = size // STEPS

    def advance(c):
        forward(c, 0, 0, 0, up).wait_recv()
        for way, source, target, device, condition in forwards:
            when(condition, lambda: forward(c, way, source, target, device).start())
        pl.when(leaving & (c % routes == last))(lambda: forward(c, 2, 0, 3, after).start())
        pl.when(leaving & (c % routes != last))(lambda: relay_in(c, blk.at[0]).start())

    def pass_on(c):
        @pl.when(relay_later & (c % routes == xi))
        def _():
            relay_in(c, own).wait_recv()
            relay_out(c // routes).start()

    def enter(c):
        @pl.when(entered_on)
        def _():
            forward(c, 0, 3, 3, up).wait_recv()
            forward(c, *entered).start()

    def arrive_near(c):
        for slot in (1, 2):
            forward(c, 0, slot, slot, up).wait_recv()

    def arrive_far(c):
        pl.when(has_before & jnp.logical_not(entered_on))(lambda: forward(c, 0, 3, 3, up).wait_recv())
        pl.when(homes_if[4])(lambda: forward(c, 0, 4, 4, up).wait_recv())

    def go(first, end):
        @pl.loop(first, end)
        def _(i):
            pl.when(i < CHUNKS)(lambda: advance(i))
            pl.when(i + FLYING < CHUNKS)(lambda: first_copy(i + FLYING, 0, zsend).start())
            pl.when((i >= 1) & (i <= CHUNKS))(lambda: pass_on(i - 1))
            pl.when((i >= 2) & (i <= CHUNKS + 1))(lambda: enter(i - 2))

    def near(k):
        pl.loop(k * CHUNKS // STEPS, (k + 1) * CHUNKS // STEPS)(arrive_near)

    def distant(k):
        pl.loop(k * CHUNKS // STEPS, (k + 1) * CHUNKS // STEPS)(arrive_far)

    def compute(k, first, end):
        @pl.loop(first, end)
        def _(p):
            left, right = pick(lefts, p), pick(rights, p)
            tile(left, right, k * step, step, 0, (k + 1) * step)
            if k:
                tile(left, right, 0, k * step, k * step, step)

    third = CHUNKS // STEPS
    go(0, third + 4)
    near(0)
    distant(0)
    compute(0, 0, pairs)
    go(third + 4, 2 * third + 2)
    near(1)
    compute(1, 0, inner)
    go(2 * third + 2, 2 * third + 4)
    distant(1)
    compute(1, inner, pairs)
    go(2 * third + 4, 3 * third + 2)
    near(2)
    compute(2, 0, inner)
    distant(2)
    compute(2, inner, pairs)

    for slot in (3, 4, 1, 2, 0):

        @functools.partial(when, homes_if[slot])
        def _(slot=slot):
            if slot < 3:
                best = jnp.max(colacc[slot], axis=0, keepdims=True)
            for g in range(size // LANES):
                lanes = slice(g * LANES, (g + 1) * LANES)
                if slot != 2:
                    across = jnp.max(rowacc[slot, lanes, :].T, axis=0, keepdims=True)
                if slot > 2:
                    rout[slot, :, lanes] = across
                elif slot == 2:
                    rout[slot, :, lanes] = best[:, lanes]
                else:
                    rout[slot, :, lanes] = jnp.maximum(best[:, lanes], across)
            result_copy(slot).start()

    @pl.loop(0, CHUNKS)
    def _(c):
        first_copy(c, 0, zsend).wait_send()
        pl.when(crossing & (c % routes == last))(lambda: first_copy(c, 3, bsend).wait_send())
        pl.when(crossing & (c % routes != last))(lambda: relay_in(c, own).wait_send())
        pl.when(leaving & (c % routes == last))(lambda: forward(c, 2, 0, 3, after).wait_send())
        pl.when(leaving & (c % routes != last))(lambda: relay_in(c, blk.at[0]).wait_send())
        pl.when(entered_on)(lambda: forward(c, *entered).wait_send())
        for way, source, target, device, condition in forwards:
            when(condition, lambda: forward(c, way, source, target, device).wait_send())

    for turn in range(CHUNKS // routes):
        pl.when(relay)(lambda turn=turn: relay_out(turn).wait_send())
    for slot in range(SLOTS):
        when(needed_if[slot], lambda slot=slot: key_copy(slot).wait_send())

    for slot in range(SLOTS):

        @functools.partial(when, needed_if[slot])
        def _(slot=slot):
            result_copy(slot).wait_recv()
            if slot:
                rin[0] = jnp.maximum(rin[0], rin[slot])

    out_ref[...] = jnp.where(valid, rin[0], -1.0).reshape(size)
    for slot in range(SLOTS):
        when(homes_if[slot], lambda slot=slot: result_copy(slot).wait_send())


def solution(mesh):
    rows, cols = mesh.shape["row"], mesh.shape["col"]
    routes = cols // 8

    def local(embeddings, doc_ids, valid_counts):
        size, depth = embeddings.shape
        vmem = pl.BlockSpec(memory_space=pltpu.VMEM)
        nearest = pl.pallas_call(
            functools.partial(kernel, rows, cols),
            out_shape=jax.ShapeDtypeStruct((size,), jnp.float32),
            in_specs=[pl.BlockSpec(memory_space=pltpu.HBM), vmem, pl.BlockSpec(memory_space=pltpu.SMEM)],
            out_specs=vmem,
            scratch_shapes=[
                pltpu.VMEM((size, depth), jnp.bfloat16),
                pltpu.SemaphoreType.DMA((CHUNKS,)),
                pltpu.VMEM((size, depth), jnp.bfloat16),
                pltpu.VMEM((CHUNKS // routes, size // CHUNKS, depth), jnp.bfloat16),
                pltpu.VMEM((SLOTS, size, depth), jnp.bfloat16),
                pltpu.VMEM((1, size), jnp.int32),
                pltpu.VMEM((SLOTS, 1, size), jnp.int32),
                pltpu.VMEM((SLOTS, size, LANES), jnp.int32),
                pltpu.VMEM((SLOTS, size, LANES), jnp.float32),
                pltpu.VMEM((SLOTS, 8, size), jnp.float32),
                pltpu.VMEM((SLOTS, 1, size), jnp.float32),
                pltpu.VMEM((SLOTS, 1, size), jnp.float32),
                pltpu.SemaphoreType.DMA((CHUNKS,)),
                pltpu.SemaphoreType.DMA((CHUNKS,)),
                pltpu.SemaphoreType.DMA((CHUNKS // routes,)),
                pltpu.SemaphoreType.DMA((CHUNKS // routes,)),
                pltpu.SemaphoreType.DMA((SLOTS, CHUNKS)),
                pltpu.SemaphoreType.DMA((SLOTS, CHUNKS)),
                pltpu.SemaphoreType.DMA((SLOTS,)),
                pltpu.SemaphoreType.DMA((SLOTS,)),
                pltpu.SemaphoreType.DMA((SLOTS,)),
                pltpu.SemaphoreType.DMA((SLOTS,)),
            ],
            compiler_params=pltpu.CompilerParams(
                collective_id=0, has_side_effects=True, vmem_limit_bytes=48 * 2**20
            ),
            cost_estimate=pl.CostEstimate(
                flops=10 * size * size * depth, bytes_accessed=4 * size * depth, transcendentals=0
            ),
        )(embeddings, doc_ids, valid_counts)
        return nearest

    in_specs = (P(("row", "col"), None), P(("row", "col")), P(("row", "col")))
    return jax.shard_map(
        local, mesh=mesh, in_specs=in_specs, out_specs=P(("row", "col")), check_vma=False
    )
```

```python
import functools

import jax
import jax.numpy as jnp
from jax import lax
from jax.experimental import pallas as pl
from jax.experimental.pallas import tpu as pltpu
from jax.sharding import PartitionSpec as P

MESH = pl.DeviceIdType.MESH
FAR = 2**30
CHUNKS = 12
STEPS = 3
SLOTS = 5
LANES = 128

PAIRS = (
    (
        ((0, 0), (0, 2), (0, 1), (3, 0), (4, 2)),
        ((0, 0), (0, 2), (1, 2), (3, 0), (3, 1)),
        ((0, 0), (0, 2), (1, 2), (3, 0), (3, 1)),
        ((0, 0), (3, 0), (3, 1), (3, 2), (4, 2)),
    ),
    (
        ((0, 0), (0, 2), (1, 2), (0, 1), (3, 0)),
        ((0, 0), (0, 2), (3, 0), (3, 1), (4, 1)),
        ((0, 0), (0, 2), (3, 0), (3, 1), (4, 1)),
        ((0, 0), (1, 2), (3, 0), (3, 1), (3, 2)),
    ),
)
FLYING = 3


def host_of(block, planes, cols):
    row, col = block // cols, block % cols
    zlo, core = row // 2, row % 2
    plane = (zlo + planes // 2 + planes * ((zlo + core) % 2)) % (2 * planes)
    half = (col // 4) % 2
    return (plane % planes) * 2 + half, (col // 8) * 8 + (plane // planes) * 4 + col % 4


def kernel(
    rows, cols, emb_hbm, ids_ref, count_ref, out_ref,
    emb_ref, esem, own, relayed, blk, kown, kin, kcol, rowacc, colacc, rout, rin,
    zsend, bsend, msend, mrecv, fsend, recv, ksend, krecv, rsend, rrecv,
):
    planes, total = rows // 2, rows * cols
    size, depth = emb_hbm.shape
    piece = size // CHUNKS
    row, col = lax.axis_index("row"), lax.axis_index("col")
    me = row * cols + col
    core, y, xi, half = row % 2, col % 4, col // 8, (col // 4) % 2
    level = (half * planes + row // 2 + 2 * planes - planes // 2) % (2 * planes)
    held_core = (level % planes + level // planes) % 2
    held = ((level % planes) * 2 + held_core) * cols + xi * 8 + core * 4 + y

    def host(block):
        return host_of(block, planes, cols)

    def home(block):
        return block // cols, block % cols

    has_next = me + 4 < total
    needed = (
        host(me),
        host(me - y + (y + 1) % 4),
        host(me - y + (y + 3) % 4),
        host(me + 4),
        host(me + 4 - half * (y - (y + 1) % 4) - (1 - half)),
    )
    needed_if = (None, None, None, has_next, has_next & (y >= 2))
    homes = (
        home(held),
        home(held - y + (y + 3) % 4),
        home(held - y + (y + 1) % 4),
        home(held - 4),
        home(held - 4 + core - (1 - core) * (y - (y + 3) % 4)),
    )
    has_before = held >= 4
    far_in = jnp.where(core == 0, (y == 0) | (y == 3), (y == 1) | (y == 2))
    homes_if = (None, None, None, has_before, has_before & far_in)
    routes = cols // 8
    last = routes - 1
    crossing = (xi == last) & (half == 1) & (core == 0)
    leaving = (xi == last) & (core == 1) & (held_core == 1) & (held + 4 < total)
    relay_first = (xi < last) & (half == 1) & (core == 0)
    relay_next = held + (last - xi) * 8 + 4
    relay_later = (xi < last) & (core == 1) & (held_core == 1) & (relay_next < total)
    relay = relay_first | relay_later
    relay_to = host(jnp.where(core == 0, me + (last - xi) * 8 + 4, relay_next))
    entering = (core == 0) & (xi == 0) & has_before
    up, down = host(held - y + (y + 1) % 4), host(held - y + (y + 3) % 4)
    after, before = host(held + 4), host(held - 4)
    far = host(held + 4 - core * (y - (y + 1) % 4) - (1 - core))
    has_after = held + 4 < total
    passes = has_after & jnp.logical_not((core == 1) & (xi == last))

    def when(condition, act):
        if condition is None:
            act()
        else:
            pl.when(condition)(act)

    def one_if(condition):
        return condition.astype(jnp.int32)

    barrier = pltpu.get_barrier_semaphore()

    def part(c):
        return pl.ds(pl.multiple_of(c * piece, piece), piece)

    def load(c):
        return pltpu.make_async_copy(emb_hbm.at[part(c)], emb_ref.at[part(c)], esem.at[c])


    def greet(device):
        pl.semaphore_signal(barrier, inc=1, device_id=device, device_id_type=MESH)

    for slot in range(SLOTS):
        when(needed_if[slot], functools.partial(greet, needed[slot]))
        when(homes_if[slot], functools.partial(greet, homes[slot]))
    greet(up)
    greet(down)
    when(has_after, functools.partial(greet, after))
    when(has_before, functools.partial(greet, before))
    greet_far_from = host(held - 4 + core - (1 - core) * (y - (y + 3) % 4))
    when(passes & (y >= 2), functools.partial(greet, far))
    far_from = homes_if[4] & jnp.logical_not(entering)
    when(far_from, functools.partial(greet, greet_far_from))

    def lane(k):
        return row, col - (xi - k) * 8

    for k in range(last):
        when(crossing | leaving, functools.partial(greet, lane(k)))
    when(relay, functools.partial(greet, lane(last)))
    when(relay, functools.partial(greet, relay_to))
    entry_row = jnp.where(held_core == 1, homes[3][0], before[0])
    entry_col = jnp.where(held_core == 1, homes[3][1], before[1])
    for k in range(last):
        when(entering, functools.partial(greet, (entry_row, entry_col - (last - k) * 8)))

    greetings = (
        8
        + one_if(needed_if[3]) + one_if(needed_if[4]) + one_if(homes_if[3]) + one_if(homes_if[4])
        + one_if(has_after) + one_if(has_before) + one_if(passes & (y >= 2)) + one_if(far_from)
        + last * one_if(crossing | leaving) + 2 * one_if(relay) + last * one_if(entering)
    )

    pl.loop(0, CHUNKS)(lambda c: load(c).start())
    places = lax.broadcasted_iota(jnp.int32, (1, size), 1)
    valid = places < count_ref[0]
    kown[...] = jnp.where(valid, ids_ref[...].reshape(1, size), FAR)
    rowacc[...] = jnp.full(rowacc.shape, -1.0, jnp.float32)
    colacc[...] = jnp.full(colacc.shape, -1.0, jnp.float32)
    pl.semaphore_wait(barrier, greetings)

    def key_copy(slot):
        return pltpu.make_async_remote_copy(
            src_ref=kown, dst_ref=kin.at[slot], send_sem=ksend.at[slot], recv_sem=krecv.at[slot],
            device_id=needed[slot], device_id_type=MESH,
        )

    def result_copy(slot):
        return pltpu.make_async_remote_copy(
            src_ref=rout.at[slot], dst_ref=rin.at[slot], send_sem=rsend.at[slot], recv_sem=rrecv.at[slot],
            device_id=homes[slot], device_id_type=MESH,
        )

    def first_copy(c, slot, sems):
        return pltpu.make_async_remote_copy(
            src_ref=own.at[part(c)], dst_ref=blk.at[slot, part(c)], send_sem=sems.at[c],
            recv_sem=recv.at[slot, c], device_id=needed[slot], device_id_type=MESH,
        )

    def forward(c, way, source, target, device):
        return pltpu.make_async_remote_copy(
            src_ref=blk.at[source, part(c)], dst_ref=blk.at[target, part(c)], send_sem=fsend.at[way, c],
            recv_sem=recv.at[target, c], device_id=device, device_id_type=MESH,
        )

    forwards = (
        (0, 0, 1, up, None),
        (1, 0, 2, down, None),
        (2, 0, 3, after, passes),
        (3, 0, 4, far, passes & (y >= 2)),
    )
    entered = (4, 3, 4, up)
    entered_on = entering & (y >= 2)

    def relay_in(c, source):
        k, turn = c % routes, c // routes
        return pltpu.make_async_remote_copy(
            src_ref=source.at[part(c)], dst_ref=relayed.at[turn], send_sem=bsend.at[c],
            recv_sem=mrecv.at[turn], device_id=(row, col - (xi - k) * 8), device_id_type=MESH,
        )

    def relay_out(turn):
        c = turn * routes + xi
        return pltpu.make_async_remote_copy(
            src_ref=relayed.at[turn], dst_ref=blk.at[3, part(c)], send_sem=msend.at[turn],
            recv_sem=recv.at[3, c], device_id=relay_to, device_id_type=MESH,
        )

    for slot in range(SLOTS):
        when(needed_if[slot], lambda slot=slot: key_copy(slot).start())

    @pl.loop(0, CHUNKS)
    def _(c):
        load(c).wait()
        floats = emb_ref[part(c), :].astype(jnp.float32)
        sums = jnp.sum(floats * floats, axis=-1, keepdims=True)
        own[part(c), :] = (floats * lax.rsqrt(sums + 1e-06)).astype(jnp.bfloat16)
        pl.when(c < FLYING)(lambda: first_copy(c, 0, zsend).start())
        pl.when(crossing & (c % routes == last))(lambda: first_copy(c, 3, bsend).start())
        pl.when(crossing & (c % routes != last))(lambda: relay_in(c, own).start())

    for turn in range(CHUNKS // routes):

        @pl.when(relay_first)
        def _(turn=turn):
            relay_in(turn * routes, own).wait_recv()
            relay_out(turn).start()

    lefts, rights = [], []
    for p in range(SLOTS):
        for side, kept in ((0, lefts), (1, rights)):
            value = jnp.int32(PAIRS[0][0][p][side])
            for k in range(2):
                for j in range(4):
                    other = PAIRS[k][j][p][side]
                    value = jnp.where((core == k) & (y == j), other, value)
            kept.append(value)
    inner = jnp.where(core == 0, jnp.where(y == 3, 1, 3), jnp.where(y == 0, 4, 2))
    pairs = jnp.where(has_before, SLOTS, inner)

    def pick(values, p):
        value = values[0]
        for k in range(1, SLOTS):
            value = jnp.where(p == k, values[k], value)
        return value

    def tile(left, right, i, count, j, width):
        scores = lax.dot_general(
            blk[left, i : i + count, :], blk[right, j : j + width, :],
            (((1,), (1,)), ((), ())), preferred_element_type=jnp.float32,
        )
        mine = kcol[left, i : i + count, :]
        best = rowacc[left, i : i + count, :]
        for g in range(width // LANES):
            lanes = slice(j + g * LANES, j + (g + 1) * LANES)
            part_scores = scores[:, g * LANES : (g + 1) * LANES]
            theirs = kin[right, :, lanes]
            best = jnp.maximum(best, jnp.where(theirs < mine, part_scores, -1.0))
            upper = jnp.where(mine < theirs, part_scores, -1.0)
            upper = jnp.max(upper.reshape(count // 8, 8, LANES), axis=0)
            colacc[right, :, lanes] = jnp.maximum(colacc[right, :, lanes], upper)
        rowacc[left, i : i + count, :] = best

    step = size // STEPS

    def advance(c):
        forward(c, 0, 0, 0, up).wait_recv()
        for way, source, target, device, condition in forwards:
            when(condition, lambda: forward(c, way, source, target, device).start())
        pl.when(leaving & (c % routes == last))(lambda: forward(c, 2, 0, 3, after).start())
        pl.when(leaving & (c % routes != last))(lambda: relay_in(c, blk.at[0]).start())

    def pass_on(c):
        @pl.when(relay_later & (c % routes == xi))
        def _():
            relay_in(c, own).wait_recv()
            relay_out(c // routes).start()

    def enter(c):
        @pl.when(entered_on)
        def _():
            forward(c, 0, 3, 3, up).wait_recv()
            forward(c, *entered).start()

    def arrive_near(c):
        for slot in (1, 2):
            forward(c, 0, slot, slot, up).wait_recv()

    def arrive_far(c):
        pl.when(has_before & jnp.logical_not(entered_on))(lambda: forward(c, 0, 3, 3, up).wait_recv())
        pl.when(homes_if[4])(lambda: forward(c, 0, 4, 4, up).wait_recv())

    def go(first, end):
        @pl.loop(first, end)
        def _(i):
            pl.when(i < CHUNKS)(lambda: advance(i))
            pl.when(i + FLYING < CHUNKS)(lambda: first_copy(i + FLYING, 0, zsend).start())
            pl.when((i >= 1) & (i <= CHUNKS))(lambda: pass_on(i - 1))
            pl.when((i >= 2) & (i <= CHUNKS + 1))(lambda: enter(i - 2))

    def near(k):
        pl.loop(k * CHUNKS // STEPS, (k + 1) * CHUNKS // STEPS)(arrive_near)

    def distant(k):
        pl.loop(k * CHUNKS // STEPS, (k + 1) * CHUNKS // STEPS)(arrive_far)

    def compute(k, first, end):
        @pl.loop(first, end)
        def _(p):
            left, right = pick(lefts, p), pick(rights, p)
            tile(left, right, k * step, step, 0, (k + 1) * step)
            if k:
                tile(left, right, 0, k * step, k * step, step)

    third = CHUNKS // STEPS
    go(0, third + 4)

    for slot in range(SLOTS):

        @functools.partial(when, homes_if[slot])
        def _(slot=slot):
            key_copy(slot).wait_recv()
            for g in range(size // LANES):
                lanes = slice(g * LANES, (g + 1) * LANES)
                kcol[slot, lanes, :] = jnp.broadcast_to(kin[slot, :, lanes], (LANES, LANES)).T

    near(0)
    distant(0)
    compute(0, 0, pairs)
    go(third + 4, 2 * third + 2)
    near(1)
    compute(1, 0, inner)
    go(2 * third + 2, 2 * third + 4)
    distant(1)
    compute(1, inner, pairs)
    go(2 * third + 4, 3 * third + 2)
    near(2)
    compute(2, 0, inner)
    distant(2)
    compute(2, inner, pairs)

    for slot in (3, 4, 1, 2, 0):

        @functools.partial(when, homes_if[slot])
        def _(slot=slot):
            if slot < 3:
                best = jnp.max(colacc[slot], axis=0, keepdims=True)
            for g in range(size // LANES):
                lanes = slice(g * LANES, (g + 1) * LANES)
                if slot != 2:
                    across = jnp.max(rowacc[slot, lanes, :].T, axis=0, keepdims=True)
                if slot > 2:
                    rout[slot, :, lanes] = across
                elif slot == 2:
                    rout[slot, :, lanes] = best[:, lanes]
                else:
                    rout[slot, :, lanes] = jnp.maximum(best[:, lanes], across)
            result_copy(slot).start()

    @pl.loop(0, CHUNKS)
    def _(c):
        first_copy(c, 0, zsend).wait_send()
        pl.when(crossing & (c % routes == last))(lambda: first_copy(c, 3, bsend).wait_send())
        pl.when(crossing & (c % routes != last))(lambda: relay_in(c, own).wait_send())
        pl.when(leaving & (c % routes == last))(lambda: forward(c, 2, 0, 3, after).wait_send())
        pl.when(leaving & (c % routes != last))(lambda: relay_in(c, blk.at[0]).wait_send())
        pl.when(entered_on)(lambda: forward(c, *entered).wait_send())
        for way, source, target, device, condition in forwards:
            when(condition, lambda: forward(c, way, source, target, device).wait_send())

    for turn in range(CHUNKS // routes):
        pl.when(relay)(lambda turn=turn: relay_out(turn).wait_send())
    for slot in range(SLOTS):
        when(needed_if[slot], lambda slot=slot: key_copy(slot).wait_send())

    for slot in range(SLOTS):

        @functools.partial(when, needed_if[slot])
        def _(slot=slot):
            result_copy(slot).wait_recv()
            if slot:
                rin[0] = jnp.maximum(rin[0], rin[slot])

    out_ref[...] = jnp.where(valid, rin[0], -1.0).reshape(size)
    for slot in range(SLOTS):
        when(homes_if[slot], lambda slot=slot: result_copy(slot).wait_send())


def solution(mesh):
    rows, cols = mesh.shape["row"], mesh.shape["col"]
    routes = cols // 8

    def local(embeddings, doc_ids, valid_counts):
        size, depth = embeddings.shape
        vmem = pl.BlockSpec(memory_space=pltpu.VMEM)
        nearest = pl.pallas_call(
            functools.partial(kernel, rows, cols),
            out_shape=jax.ShapeDtypeStruct((size,), jnp.float32),
            in_specs=[pl.BlockSpec(memory_space=pltpu.HBM), vmem, pl.BlockSpec(memory_space=pltpu.SMEM)],
            out_specs=vmem,
            scratch_shapes=[
                pltpu.VMEM((size, depth), jnp.bfloat16),
                pltpu.SemaphoreType.DMA((CHUNKS,)),
                pltpu.VMEM((size, depth), jnp.bfloat16),
                pltpu.VMEM((CHUNKS // routes, size // CHUNKS, depth), jnp.bfloat16),
                pltpu.VMEM((SLOTS, size, depth), jnp.bfloat16),
                pltpu.VMEM((1, size), jnp.int32),
                pltpu.VMEM((SLOTS, 1, size), jnp.int32),
                pltpu.VMEM((SLOTS, size, LANES), jnp.int32),
                pltpu.VMEM((SLOTS, size, LANES), jnp.float32),
                pltpu.VMEM((SLOTS, 8, size), jnp.float32),
                pltpu.VMEM((SLOTS, 1, size), jnp.float32),
                pltpu.VMEM((SLOTS, 1, size), jnp.float32),
                pltpu.SemaphoreType.DMA((CHUNKS,)),
                pltpu.SemaphoreType.DMA((CHUNKS,)),
                pltpu.SemaphoreType.DMA((CHUNKS // routes,)),
                pltpu.SemaphoreType.DMA((CHUNKS // routes,)),
                pltpu.SemaphoreType.DMA((SLOTS, CHUNKS)),
                pltpu.SemaphoreType.DMA((SLOTS, CHUNKS)),
                pltpu.SemaphoreType.DMA((SLOTS,)),
                pltpu.SemaphoreType.DMA((SLOTS,)),
                pltpu.SemaphoreType.DMA((SLOTS,)),
                pltpu.SemaphoreType.DMA((SLOTS,)),
            ],
            compiler_params=pltpu.CompilerParams(
                collective_id=0, has_side_effects=True, vmem_limit_bytes=48 * 2**20
            ),
            cost_estimate=pl.CostEstimate(
                flops=10 * size * size * depth, bytes_accessed=4 * size * depth, transcendentals=0
            ),
        )(embeddings, doc_ids, valid_counts)
        return nearest

    in_specs = (P(("row", "col"), None), P(("row", "col")), P(("row", "col")))
    return jax.shard_map(
        local, mesh=mesh, in_specs=in_specs, out_specs=P(("row", "col")), check_vma=False
    )
```
